32 devices in a mesh: dp: 2 (over core), seq: 4 (over z), expert: 4 (over y, x).
Axes of the slice: x: 2, y: 2, z: 4, core: 2. Of those that a mesh axis runs over, the one named last changes fastest.
Arguments:
- tokens: bfloat16 [8192, 2048], P(('dp', 'seq')), may hold values from -6 to 6
- phi: bfloat16 [2048, 8], P(None, 'expert'), may hold values from -40 to 40
- w_in: bfloat16 [8, 2048, 8192], P('expert', None, ('dp', 'seq')), may hold values from -1 to 1
- w_out: bfloat16 [8, 8192, 2048], P('expert', ('dp', 'seq')), may hold values from -0.25 to 0.25
Outputs:
- mixed: bfloat16 [8192, 2048], P(('dp', 'seq', 'expert'))
The draws below stay inside these ranges and needn't reach their ends.
All inputs are finite; a program needn't handle non-finite values.
Results may differ from the reference program's by a relative error of at most 0.0068.
Values may be sent and summed in bfloat16 or wider, within the bound.
No kernel may reach another device: no remote copies, remote signals or barrier semaphores. Data moves between devices by JAX's collectives and lax.ppermute only.
A program may use at most 64 MiB of HBM per device.

```python
import jax
import jax.numpy as jnp
from jax import lax

D = 2048
FF = 8192
EXPERTS = 8
LENGTH = 4096
CLIPS = 2
TOKENS = 8192


def drawn(key):
    base_key = jax.random.fold_in(key, 7)
    key_tok, key_phi = jax.random.split(base_key, 2)
    tokens = jnp.clip(jax.random.normal(key_tok, (TOKENS, D), jnp.float32), -5.0, 5.0)
    phi = jax.random.normal(key_phi, (D, EXPERTS), jnp.float32) * (2.0 / jnp.sqrt(jnp.float32(D)))
    return (tokens, phi)


def draw_tokens(key, part):
    return drawn(key)[0].astype(jnp.bfloat16)


def draw_phi(key, part):
    return drawn(key)[1].astype(jnp.bfloat16)


def levels(rng, dims, cuts, smallest, high):
    gain, own = 1.0, jax.random.fold_in(rng, 6)
    for dim, blocks in cuts:
        draws = jnp.exp(jax.random.uniform(jax.random.fold_in(own, dim), (blocks,), jnp.float32, smallest / len(cuts), high / len(cuts)))
        gain = gain * jnp.repeat(draws, dims[dim] // blocks).reshape([-1 if axis == dim else 1 for axis in range(len(dims))])
    return gain


def normal_values(stream_key, shape, scale, most, shards=(), dtype=jnp.bfloat16):
    drawn = jax.random.normal(stream_key, shape, jnp.float32) * scale
    if len(shards) > 0:
        drawn = levels(stream_key, shape, shards, -0.22, 0.18) * drawn
    return jnp.clip(drawn, min=-most, max=most).astype(dtype)


def setup_inputs(seed: int = 0) -> dict:
    arg_keys = jax.random.split(jax.random.key(seed), 5)
    return {
        "tokens": draw_tokens(jax.random.fold_in(arg_keys[4], 71), 0),
        "phi": draw_phi(jax.random.fold_in(arg_keys[4], 71), 0),
        "w_in": normal_values(arg_keys[2], (EXPERTS, D, FF), (D // 64) ** -0.5, 1.0, ((0, 4), (2, 8))),
        "w_out": normal_values(arg_keys[3], (EXPERTS, FF, D), (FF // 16) ** -0.5, 0.25, ((0, 4), (1, 8))),
    }


def expert_layer(packed):
    inputs, first, second = packed
    hidden = jax.nn.gelu(jnp.dot(inputs, first, preferred_element_type=jnp.float32), approximate=True).astype(jnp.bfloat16)
    return jnp.dot(hidden, second, preferred_element_type=jnp.float32).astype(jnp.bfloat16)


def reference(tokens, phi, w_in, w_out):
    clip_rows = tokens.reshape(CLIPS, LENGTH, D)
    logits = jnp.stack([lax.dot_general(phi, clip_rows[clip_index], (((0,), (1,)), ((), ())), preferred_element_type=jnp.float32) for clip_index in range(CLIPS)])
    slot_max = jnp.max(logits, axis=2, keepdims=True)
    spread = jnp.exp(logits - slot_max)
    spread_b = spread.astype(jnp.bfloat16)
    numerator = jnp.stack([jnp.dot(spread_b[clip_index], clip_rows[clip_index], preferred_element_type=jnp.float32) for clip_index in range(CLIPS)])
    denominator = jnp.sum(spread, axis=2)
    slot_in = (numerator / denominator[:, :, None]).astype(jnp.bfloat16)
    slot_out = lax.map(expert_layer, (jnp.transpose(slot_in, (1, 0, 2)), w_in, w_out))
    slot_out = jnp.transpose(slot_out, (1, 0, 2))
    row_max = jnp.max(logits, axis=1, keepdims=True)
    weight = jnp.exp(logits - row_max)
    weight_b = weight.astype(jnp.bfloat16)
    outputs = []
    for clip_index in range(CLIPS):
        summed = lax.dot_general(weight_b[clip_index], slot_out[clip_index], (((0,), (0,)), ((), ())), preferred_element_type=jnp.float32)
        totals = jnp.sum(weight[clip_index], axis=0)
        outputs.append((summed / totals[:, None]).astype(jnp.bfloat16))
    return jnp.concatenate(outputs, axis=0)
```

```python
import functools

import jax
import jax.numpy as jnp
from jax import lax
from jax.experimental import pallas as pl
from jax.experimental.pallas import tpu as pltpu
from jax.sharding import PartitionSpec as P

F32, BF16 = jnp.float32, jnp.bfloat16
LANES = 128
VMEM = pl.BlockSpec(memory_space=pltpu.VMEM)


def params(mib):
    return pltpu.CompilerParams(vmem_limit_bytes=mib << 20)


def partners(n, step):
    if n & (n - 1):
        return [(i, (i + step) % n) for i in range(n)]
    return [(i, i ^ step) for i in range(n)]


def gathered(x, axis, n):
    return [x] + [lax.ppermute(x, axis, partners(n, step)) for step in range(1, n)]


def slot_sums_kernel(chunks, phi_ref, tokens_ref, packed_ref, logits_ref, held, sems):
    rows, width = tokens_ref.shape[0] // chunks, tokens_ref.shape[1]

    def copy(c):
        part = pl.ds(c * rows, rows)
        return pltpu.make_async_copy(tokens_ref.at[part], held.at[part], sems.at[c])

    for c in range(chunks):
        copy(c).start()
    phi = phi_ref[...].T
    tops, sums, totals = [], [], []
    for c in range(chunks):
        copy(c).wait()
        part = held[pl.ds(c * rows, rows), :]
        logits = lax.dot_general(phi, part, (((1,), (1,)), ((), ())), preferred_element_type=F32)
        logits_ref[:, pl.ds(c * rows, rows)] = logits
        top = jnp.max(logits, axis=1, keepdims=True)
        spread = jnp.exp(logits - top)
        tops.append(top)
        totals.append(jnp.sum(spread, axis=1, keepdims=True))
        sums.append(jnp.dot(spread.astype(BF16), part, preferred_element_type=F32))
    top = functools.reduce(jnp.maximum, tops)
    scales = [jnp.exp(t - top) for t in tops]
    packed_ref[:, :width] = sum(s * v for s, v in zip(scales, sums))
    total = sum(s * v for s, v in zip(scales, totals))
    lane = lax.broadcasted_iota(jnp.int32, (top.shape[0], LANES), 1)
    packed_ref[:, width:] = jnp.where(lane == 0, top, total)


def slot_sums(phi, tokens, chunks=4):
    slots, (count, width) = phi.shape[1], tokens.shape
    return pl.pallas_call(
        functools.partial(slot_sums_kernel, chunks),
        out_shape=(
            jax.ShapeDtypeStruct((slots, width + LANES), F32),
            jax.ShapeDtypeStruct((slots, count), F32),
        ),
        in_specs=[VMEM, pl.BlockSpec(memory_space=pl.ANY)],
        out_specs=(VMEM, VMEM),
        scratch_shapes=[pltpu.VMEM(tokens.shape, BF16), pltpu.SemaphoreType.DMA((chunks,))],
        compiler_params=params(16),
    )(phi, tokens)


def slot_inputs_kernel(*refs):
    *packed, out_ref = refs
    width = out_ref.shape[1]
    tops = [p[:, width : width + 1] for p in packed]
    top = functools.reduce(jnp.maximum, tops)
    scales = [jnp.exp(t - top) for t in tops]
    total = sum(s * p[:, width + 1 : width + 2] for s, p in zip(scales, packed))
    out_ref[...] = sum(s * p[:, :width] for s, p in zip(scales, packed)) / total


def slot_inputs(packed):
    slots, wide = packed[0].shape
    return pl.pallas_call(
        slot_inputs_kernel,
        out_shape=jax.ShapeDtypeStruct((slots, wide - LANES), F32),
        in_specs=[VMEM] * len(packed),
        out_specs=VMEM,
        cost_estimate=pl.CostEstimate(flops=10_000_000_000, bytes_accessed=0, transcendentals=0),
        compiler_params=params(4),
    )(*packed)


def gelu(v):
    return 0.5 * v * (1.0 + jnp.tanh(0.7978845608028654 * (v + 0.044715 * v * v * v)))


def experts_kernel(clips, *refs):
    x_refs, (first_ref, second_ref), out_refs = refs[:clips], refs[clips:-clips], refs[-clips:]
    for e in range(first_ref.shape[0]):
        x = jnp.concatenate([x_ref[e : e + 1, :] for x_ref in x_refs], axis=0).astype(BF16)
        hidden = gelu(jnp.dot(x, first_ref[e], preferred_element_type=F32)).astype(BF16)
        value = jnp.dot(hidden, second_ref[e], preferred_element_type=F32)
        for c in range(clips):
            out_refs[c][e : e + 1, :] = value[c : c + 1, :]


def experts(slot_in, w_in, w_out):
    clips = len(slot_in)
    return pl.pallas_call(
        functools.partial(experts_kernel, clips),
        out_shape=[jax.ShapeDtypeStruct(x.shape, F32) for x in slot_in],
        in_specs=[VMEM] * (clips + 2),
        out_specs=[VMEM] * clips,
        compiler_params=params(4),
    )(*slot_in, w_in, w_out)


def pack_kernel(*refs):
    *values, logits_ref, out_ref = refs
    width = values[0].shape[1]
    out_ref[:, :width] = sum(v[...] for v in values).astype(BF16).astype(F32)
    out_ref[:, width:] = logits_ref[...]


def pack(values, logits):
    slots, width = values[0].shape
    return pl.pallas_call(
        pack_kernel,
        out_shape=jax.ShapeDtypeStruct((slots, width + logits.shape[1]), F32),
        in_specs=[VMEM] * (len(values) + 1),
        out_specs=VMEM,
        compiler_params=params(4),
    )(*values, logits)


def mix_kernel(*refs):
    *slot_out, logits_ref, out_ref = refs
    logits = logits_ref[...]
    weight = jnp.exp(logits - jnp.max(logits, axis=0, keepdims=True))
    weight = (weight / jnp.sum(weight, axis=0, keepdims=True)).astype(BF16)
    width = out_ref.shape[1]
    values = jnp.concatenate([s[:, :width] for s in slot_out], axis=0).astype(BF16)
    out_ref[...] = lax.dot_general(
        weight, values, (((0,), (0,)), ((), ())), preferred_element_type=F32
    ).astype(BF16)


def mix(packed, logits, width):
    return pl.pallas_call(
        mix_kernel,
        out_shape=jax.ShapeDtypeStruct((logits.shape[1], width), BF16),
        in_specs=[VMEM] * (len(packed) + 1),
        out_specs=VMEM,
        compiler_params=params(8),
    )(*packed, logits)


def on_device(sizes, tokens, phi, w_in, w_out):
    cores, seqs, groups = sizes
    count, width = tokens.shape
    packed, logits = slot_sums(phi, tokens)
    own_in = slot_inputs(gathered(packed, "seq", seqs))
    slot_in = gathered(own_in, "dp", cores)
    partial = experts(slot_in, w_in, w_out)
    own = partial[0]
    for step in range(1, cores):
        own = own + lax.ppermute(partial[step], "dp", partners(cores, step))
    mine = pack(gathered(own, "seq", seqs), logits)
    everyone = gathered(mine, "expert", groups)
    rows = count // groups
    all_logits = jnp.concatenate([v[:, width:] for v in everyone], axis=0)
    first = lax.axis_index("expert") * rows
    return mix(everyone, lax.dynamic_slice_in_dim(all_logits, first, rows, axis=1), width)


def solution(mesh):
    sizes = tuple(mesh.shape[axis] for axis in ("dp", "seq", "expert"))
    placed = (
        P(("dp", "seq"), None),
        P(None, "expert"),
        P("expert", None, ("dp", "seq")),
        P("expert", ("dp", "seq"), None),
    )
    return jax.shard_map(
        functools.partial(on_device, sizes),
        mesh=mesh,
        in_specs=placed,
        out_specs=P(("dp", "seq", "expert"), None),
        check_vma=False,
    )
```

```python
import functools

import jax
import jax.numpy as jnp
from jax import lax
from jax.experimental import pallas as pl
from jax.experimental.pallas import tpu as pltpu
from jax.sharding import PartitionSpec as P

F32, BF16 = jnp.float32, jnp.bfloat16
LANES = 128
VMEM = pl.BlockSpec(memory_space=pltpu.VMEM)


def in_hbm(x):
    return pltpu.with_memory_space_constraint(x, pltpu.HBM)


def params(mib):
    return pltpu.CompilerParams(vmem_limit_bytes=mib << 20)


def partners(n, step):
    if n & (n - 1):
        return [(i, (i + step) % n) for i in range(n)]
    return [(i, i ^ step) for i in range(n)]


def gathered(x, axis, n):
    return [x] + [lax.ppermute(x, axis, partners(n, step)) for step in range(1, n)]


def slot_sums_kernel(chunks, phi_hbm, tokens_hbm, packed_ref, logits_ref, phi_ref, held, sems):
    slots, width = phi_ref.shape
    rows = tokens_hbm.shape[0] // chunks

    def copy(c):
        part = pl.ds(c * rows, rows)
        return pltpu.make_async_copy(tokens_hbm.at[part], held.at[part], sems.at[c])

    phi_copy = pltpu.make_async_copy(phi_hbm, phi_ref, sems.at[chunks])
    phi_copy.start()
    for c in range(chunks):
        copy(c).start()
    phi_copy.wait()
    spare = jnp.zeros((8 - slots % 8, width), F32)
    phi = jnp.concatenate([phi_ref[...].astype(F32), spare], axis=0).T.astype(BF16)
    tops, sums, totals = [], [], []

    def finish(c, by_token):
        part = pl.ds(c * rows, rows)
        logits = by_token.T[:slots]
        logits_ref[:, part] = logits
        top = jnp.max(logits, axis=1, keepdims=True)
        spread = jnp.exp(logits - top)
        tops.append(top)
        totals.append(jnp.sum(spread, axis=1, keepdims=True))
        sums.append(jnp.dot(spread.astype(BF16), held[part, :], preferred_element_type=F32))

    before = None
    for c in range(chunks):
        copy(c).wait()
        now = jnp.dot(held[pl.ds(c * rows, rows), :], phi, preferred_element_type=F32)
        if c:
            finish(c - 1, before)
        before = now
    finish(chunks - 1, before)
    top = functools.reduce(jnp.maximum, tops)
    scales = [jnp.exp(t - top) for t in tops]
    packed_ref[:, :width] = sum(s * v for s, v in zip(scales, sums))
    total = sum(s * v for s, v in zip(scales, totals))
    lane = lax.broadcasted_iota(jnp.int32, (slots, LANES), 1)
    packed_ref[:, width:] = jnp.where(lane == 0, top, total)


def slot_sums(phi, tokens, chunks=4):
    (slots, width), count = phi.shape, tokens.shape[0]
    return pl.pallas_call(
        functools.partial(slot_sums_kernel, chunks),
        out_shape=(
            jax.ShapeDtypeStruct((slots, width + LANES), F32),
            jax.ShapeDtypeStruct((slots, count), F32),
        ),
        in_specs=[pl.BlockSpec(memory_space=pltpu.HBM)] * 2,
        out_specs=(VMEM, VMEM),
        scratch_shapes=[
            pltpu.VMEM(phi.shape, BF16),
            pltpu.VMEM(tokens.shape, BF16),
            pltpu.SemaphoreType.DMA((chunks + 1,)),
        ],
        compiler_params=params(16),
    )(in_hbm(phi), in_hbm(tokens))


def slot_inputs_kernel(*refs):
    *packed, out_ref = refs
    width = out_ref.shape[1]
    tops = [p[:, width : width + 1] for p in packed]
    top = functools.reduce(jnp.maximum, tops)
    scales = [jnp.exp(t - top) for t in tops]
    total = sum(s * p[:, width + 1 : width + 2] for s, p in zip(scales, packed))
    out_ref[...] = sum(s * p[:, :width] for s, p in zip(scales, packed)) / total


def slot_inputs(packed):
    slots, wide = packed[0].shape
    return pl.pallas_call(
        slot_inputs_kernel,
        out_shape=jax.ShapeDtypeStruct((slots, wide - LANES), F32),
        in_specs=[VMEM] * len(packed),
        out_specs=VMEM,
        cost_estimate=pl.CostEstimate(flops=10_000_000_000, bytes_accessed=0, transcendentals=0),
        compiler_params=params(4),
    )(*packed)


def gelu(v):
    return 0.5 * v * (1.0 + jnp.tanh(0.7978845608028654 * (v + 0.044715 * v * v * v)))


def experts_kernel(clips, *refs):
    x_refs, (first_ref, second_ref), out_refs = refs[:clips], refs[clips:-clips], refs[-clips:]
    for e in range(first_ref.shape[0]):
        x = jnp.concatenate([x_ref[e : e + 1, :] for x_ref in x_refs], axis=0).astype(BF16)
        hidden = gelu(jnp.dot(x, first_ref[e], preferred_element_type=F32)).astype(BF16)
        value = jnp.dot(hidden, second_ref[e], preferred_element_type=F32)
        for c in range(clips):
            out_refs[c][e : e + 1, :] = value[c : c + 1, :]


def experts(slot_in, w_in, w_out):
    clips = len(slot_in)
    return pl.pallas_call(
        functools.partial(experts_kernel, clips),
        out_shape=[jax.ShapeDtypeStruct(x.shape, F32) for x in slot_in],
        in_specs=[VMEM] * (clips + 2),
        out_specs=[VMEM] * clips,
        compiler_params=params(4),
    )(*slot_in, w_in, w_out)


def pack_kernel(*refs):
    *values, logits_ref, out_ref = refs
    width = values[0].shape[1]
    out_ref[:, :width] = sum(v[...] for v in values).astype(BF16).astype(F32)
    out_ref[:, width:] = logits_ref[...]


def pack(values, logits):
    slots, width = values[0].shape
    return pl.pallas_call(
        pack_kernel,
        out_shape=jax.ShapeDtypeStruct((slots, width + logits.shape[1]), F32),
        in_specs=[VMEM] * (len(values) + 1),
        out_specs=VMEM,
        compiler_params=params(4),
    )(*values, logits)


def mix_kernel(chunks, *refs):
    *slot_out, logits_ref, out_hbm, rows_ref, sems = refs
    logits = logits_ref[...]
    weight = jnp.exp(logits - jnp.max(logits, axis=0, keepdims=True))
    weight = (weight / jnp.sum(weight, axis=0, keepdims=True)).astype(BF16)
    rows, width = rows_ref.shape[0] // chunks, rows_ref.shape[1]
    values = jnp.concatenate([s[:, :width] for s in slot_out], axis=0).astype(BF16)
    copies = []
    for c in range(chunks):
        part = pl.ds(c * rows, rows)
        rows_ref[part, :] = lax.dot_general(
            weight[:, c * rows : (c + 1) * rows],
            values,
            (((0,), (0,)), ((), ())),
            preferred_element_type=F32,
        ).astype(BF16)
        copies.append(pltpu.make_async_copy(rows_ref.at[part], out_hbm.at[part], sems.at[c]))
        copies[-1].start()
    for copy in copies:
        copy.wait()


def mix(packed, logits, width, chunks=4):
    shape = (logits.shape[1], width)
    return pl.pallas_call(
        functools.partial(mix_kernel, chunks),
        out_shape=jax.ShapeDtypeStruct(shape, BF16),
        in_specs=[VMEM] * (len(packed) + 1),
        out_specs=pl.BlockSpec(memory_space=pl.ANY),
        scratch_shapes=[pltpu.VMEM(shape, BF16), pltpu.SemaphoreType.DMA((chunks,))],
        compiler_params=params(8),
    )(*packed, logits)


def on_device(sizes, tokens, phi, w_in, w_out):
    cores, seqs, groups = sizes
    count, width = tokens.shape
    packed, logits = slot_sums(phi.T, tokens)
    own_in = slot_inputs(gathered(packed, "seq", seqs))
    slot_in = gathered(own_in, "dp", cores)
    partial = experts(slot_in, w_in, w_out)
    own = partial[0]
    for step in range(1, cores):
        own = own + lax.ppermute(partial[step], "dp", partners(cores, step))
    mine = pack(gathered(own, "seq", seqs), logits)
    everyone = gathered(mine, "expert", groups)
    rows = count // groups
    all_logits = jnp.concatenate([v[:, width:] for v in everyone], axis=0)
    first = lax.axis_index("expert") * rows
    return mix(everyone, lax.dynamic_slice_in_dim(all_logits, first, rows, axis=1), width)


def solution(mesh):
    sizes = tuple(mesh.shape[axis] for axis in ("dp", "seq", "expert"))
    placed = (
        P(("dp", "seq"), None),
        P(None, "expert"),
        P("expert", None, ("dp", "seq")),
        P("expert", ("dp", "seq"), None),
    )
    return jax.shard_map(
        functools.partial(on_device, sizes),
        mesh=mesh,
        in_specs=placed,
        out_specs=P(("dp", "seq", "expert"), None),
        check_vma=False,
    )
```

```python
import functools

import jax
import jax.numpy as jnp
from jax import lax
from jax.experimental import pallas as pl
from jax.experimental.pallas import tpu as pltpu
from jax.sharding import PartitionSpec as P

F32, BF16 = jnp.float32, jnp.bfloat16
LANES = 128
VMEM = pl.BlockSpec(memory_space=pltpu.VMEM)


def in_hbm(x):
    return pltpu.with_memory_space_constraint(x, pltpu.HBM)


def params(mib):
    return pltpu.CompilerParams(vmem_limit_bytes=mib << 20)


def partners(n, step):
    if n & (n - 1):
        return [(i, (i + step) % n) for i in range(n)]
    return [(i, i ^ step) for i in range(n)]


def middle_first(n):
    return sorted(range(1, n), key=lambda step: (step != n // 2, step))


def exchange(x, sizes, axis, step):
    cores, seqs, groups = sizes
    to = dict(partners(seqs if axis == "seq" else groups, step))
    pairs = []
    for core in range(cores):
        for seq in range(seqs):
            for group in range(groups):
                place = (core * seqs + seq) * groups + group
                target_seq, target_group = (to[seq], group) if axis == "seq" else (seq, to[group])
                pairs.append((place, ((core ^ 1) * seqs + target_seq) * groups + target_group))
    return lax.ppermute(x, ("dp", "seq", "expert"), pairs)


def slot_sums_kernel(chunks, phi_hbm, tokens_hbm, packed_ref, phi_ref, held, sems):
    slots, width = phi_ref.shape
    rows = tokens_hbm.shape[0] // chunks
    wide = width + LANES

    def copy(c):
        part = pl.ds(c * rows, rows)
        return pltpu.make_async_copy(tokens_hbm.at[part], held.at[part], sems.at[c])

    phi_copy = pltpu.make_async_copy(phi_hbm, phi_ref, sems.at[chunks])
    phi_copy.start()
    for c in range(chunks):
        copy(c).start()
    phi_copy.wait()
    spare = jnp.zeros((8 - slots % 8, width), F32)
    phi = jnp.concatenate([phi_ref[...].astype(F32), spare], axis=0).T.astype(BF16)
    tops, sums, totals = [], [], []

    def finish(c, by_token):
        part = pl.ds(c * rows, rows)
        logits = by_token.T[:slots]
        packed_ref[:, pl.ds(wide + c * rows, rows)] = logits
        top = jnp.max(logits, axis=1, keepdims=True)
        spread = jnp.exp(logits - top)
        tops.append(top)
        totals.append(jnp.sum(spread, axis=1, keepdims=True))
        sums.append(jnp.dot(spread.astype(BF16), held[part, :], preferred_element_type=F32))

    before = None
    for c in range(chunks):
        copy(c).wait()
        now = jnp.dot(held[pl.ds(c * rows, rows), :], phi, preferred_element_type=F32)
        if c:
            finish(c - 1, before)
        before = now
    finish(chunks - 1, before)
    top = functools.reduce(jnp.maximum, tops)
    scales = [jnp.exp(t - top) for t in tops]
    packed_ref[:, :width] = sum(s * v for s, v in zip(scales, sums))
    total = sum(s * v for s, v in zip(scales, totals))
    lane = lax.broadcasted_iota(jnp.int32, (slots, LANES), 1)
    packed_ref[:, width:wide] = jnp.where(lane == 0, top, total)


def slot_sums(phi, tokens, chunks=4):
    (slots, width), count = phi.shape, tokens.shape[0]
    return pl.pallas_call(
        functools.partial(slot_sums_kernel, chunks),
        out_shape=jax.ShapeDtypeStruct((slots, width + LANES + count), F32),
        in_specs=[pl.BlockSpec(memory_space=pltpu.HBM)] * 2,
        out_specs=VMEM,
        scratch_shapes=[
            pltpu.VMEM(phi.shape, BF16),
            pltpu.VMEM(tokens.shape, BF16),
            pltpu.SemaphoreType.DMA((chunks + 1,)),
        ],
        compiler_params=params(16),
    )(in_hbm(phi), in_hbm(tokens))


def joined(parts, width):
    tops = [p[:, width : width + 1] for p in parts]
    top = functools.reduce(jnp.maximum, tops)
    scales = [jnp.exp(t - top) for t in tops]
    total = sum(s * p[:, width + 1 : width + 2] for s, p in zip(scales, parts))
    return sum(s * p[:, :width] for s, p in zip(scales, parts)), top, total


def swapped(x):
    half = x.shape[0] // 2
    return jnp.concatenate([x[half:], x[:half]], axis=0)


def join_kernel(own_ref, *refs):
    *received, out_ref = refs
    parts = [swapped(r[...]) for r in received]
    value, _, total = joined([own_ref[...]] + parts, out_ref.shape[1])
    out_ref[...] = value / total


def join(own, received):
    slots, wide = own.shape
    return pl.pallas_call(
        join_kernel,
        out_shape=jax.ShapeDtypeStruct((slots, wide - LANES), F32),
        in_specs=[VMEM] * (len(received) + 1),
        out_specs=VMEM,
        cost_estimate=pl.CostEstimate(flops=10_000_000_000, bytes_accessed=0, transcendentals=0),
        compiler_params=params(4),
    )(own, *received)


def gelu(v):
    return 0.5 * v * (1.0 + jnp.tanh(0.7978845608028654 * (v + 0.044715 * v * v * v)))


def experts_kernel(x_ref, first_ref, second_ref, out_ref):
    slots = first_ref.shape[0]
    for e in range(slots):
        x = jnp.concatenate([x_ref[e : e + 1, :], x_ref[slots + e : slots + e + 1, :]], axis=0)
        hidden = jnp.dot(x.astype(BF16), first_ref[e], preferred_element_type=F32)
        value = jnp.dot(gelu(hidden).astype(BF16), second_ref[e], preferred_element_type=F32)
        out_ref[e : e + 1, :] = value[:1]
        out_ref[slots + e : slots + e + 1, :] = value[1:]


def experts(slot_in, w_in, w_out):
    return pl.pallas_call(
        experts_kernel,
        out_shape=jax.ShapeDtypeStruct(slot_in.shape, F32),
        in_specs=[VMEM] * 3,
        out_specs=VMEM,
        compiler_params=params(4),
    )(slot_in, w_in, w_out)


def pack_kernel(chip_ref, *refs):
    *received, logits_ref, own_ref, other_ref = refs
    slots, width = own_ref.shape[0], chip_ref.shape[1]
    total = chip_ref[...]
    for r in received:
        total += swapped(r[...])
    total = total.astype(BF16).astype(F32)
    for out_ref, part in ((own_ref, slice(0, slots)), (other_ref, slice(slots, 2 * slots))):
        out_ref[:, :width] = total[part]
        out_ref[:, width:] = logits_ref[part, :]


def pack(chip, received, logits):
    slots, width = chip.shape
    shape = jax.ShapeDtypeStruct((slots // 2, width + logits.shape[1]), F32)
    return pl.pallas_call(
        pack_kernel,
        out_shape=(shape, shape),
        in_specs=[VMEM] * (len(received) + 2),
        out_specs=(VMEM, VMEM),
        compiler_params=params(4),
    )(chip, *received, logits)


def mix_kernel(chunks, *refs):
    *packed, out_hbm, rows_ref, sems = refs
    (count, width), group = rows_ref.shape, lax.axis_index("expert")
    rows = count // chunks
    values = jnp.concatenate([p[:, :width] for p in packed], axis=0).astype(BF16)
    everything = jnp.concatenate([p[:, width:] for p in packed], axis=0)
    logits = everything[:, :count]
    for g in range(1, len(packed)):
        logits = jnp.where(group == g, everything[:, g * count : (g + 1) * count], logits)
    weight = jnp.exp(logits - jnp.max(logits, axis=0, keepdims=True))
    weight = (weight / jnp.sum(weight, axis=0, keepdims=True)).astype(BF16)
    copies = []
    for c in range(chunks):
        part = pl.ds(c * rows, rows)
        rows_ref[part, :] = lax.dot_general(
            weight[:, c * rows : (c + 1) * rows],
            values,
            (((0,), (0,)), ((), ())),
            preferred_element_type=F32,
        ).astype(BF16)
        copies.append(pltpu.make_async_copy(rows_ref.at[part], out_hbm.at[part], sems.at[c]))
        copies[-1].start()
    for copy in copies:
        copy.wait()


def mix(packed, width, chunks=4):
    shape = ((packed[0].shape[1] - width) // len(packed), width)
    return pl.pallas_call(
        functools.partial(mix_kernel, chunks),
        out_shape=jax.ShapeDtypeStruct(shape, BF16),
        in_specs=[VMEM] * len(packed),
        out_specs=pl.BlockSpec(memory_space=pl.ANY),
        scratch_shapes=[pltpu.VMEM(shape, BF16), pltpu.SemaphoreType.DMA((chunks,))],
        compiler_params=params(8),
    )(*packed)


def on_device(sizes, tokens, phi, w_in, w_out):
    cores, seqs, groups = sizes
    width = tokens.shape[1]
    swap = partners(cores, 1)
    packed = slot_sums(phi.T, tokens)
    both = jnp.concatenate([packed, lax.ppermute(packed, "dp", swap)], axis=0)
    both, logits = both[:, : width + LANES], both[:, width + LANES :]
    slot_in = join(both, [exchange(both, sizes, "seq", step) for step in range(1, seqs)])
    partial = experts(slot_in, w_in, w_out)
    chip = partial + swapped(lax.ppermute(partial, "dp", swap))
    sums = [exchange(chip, sizes, "seq", step) for step in middle_first(seqs)]
    own, other = pack(chip, sums, logits)
    everyone = [own] + [exchange(other, sizes, "expert", step) for step in range(1, groups)]
    return mix(everyone, width)


def solution(mesh):
    sizes = tuple(mesh.shape[axis] for axis in ("dp", "seq", "expert"))
    placed = (
        P(("dp", "seq"), None),
        P(None, "expert"),
        P("expert", None, ("dp", "seq")),
        P("expert", ("dp", "seq"), None),
    )
    return jax.shard_map(
        functools.partial(on_device, sizes),
        mesh=mesh,
        in_specs=placed,
        out_specs=P(("dp", "seq", "expert"), None),
        check_vma=False,
    )
```

```python
import functools

import jax
import jax.numpy as jnp
from jax import lax
from jax.experimental import pallas as pl
from jax.experimental.pallas import tpu as pltpu
from jax.sharding import PartitionSpec as P

F32, BF16 = jnp.float32, jnp.bfloat16
LANES = 128
VMEM = pl.BlockSpec(memory_space=pltpu.VMEM)


def in_hbm(x):
    return pltpu.with_memory_space_constraint(x, pltpu.HBM)


def params(mib):
    return pltpu.CompilerParams(vmem_limit_bytes=mib << 20)


def partners(n, step):
    if n & (n - 1):
        return [(i, (i + step) % n) for i in range(n)]
    return [(i, i ^ step) for i in range(n)]


def middle_first(n):
    return sorted(range(1, n), key=lambda step: (step != n // 2, step))


def exchange(x, sizes, axis, step):
    cores, seqs, groups = sizes
    to = dict(partners(seqs if axis == "seq" else groups, step))
    pairs = []
    for core in range(cores):
        for seq in range(seqs):
            for group in range(groups):
                place = (core * seqs + seq) * groups + group
                target_seq, target_group = (to[seq], group) if axis == "seq" else (seq, to[group])
                pairs.append((place, ((core ^ 1) * seqs + target_seq) * groups + target_group))
    return lax.ppermute(x, ("dp", "seq", "expert"), pairs)


def scalars(top, total):
    lane = lax.broadcasted_iota(jnp.int32, (top.shape[0], LANES), 1)
    lanes = jnp.zeros(lane.shape, F32)
    for at, rest in ((0, top), (3, total)):
        for i in range(3):
            piece = rest.astype(BF16).astype(F32)
            lanes = jnp.where(lane == at + i, piece, lanes)
            rest = rest - piece
    return lanes


def joined(parts, width):
    def scalar(part, at):
        return sum(part[:, width + at + i : width + at + i + 1] for i in range(3))

    tops = [scalar(p, 0) for p in parts]
    top = functools.reduce(jnp.maximum, tops)
    scales = [jnp.exp(t - top) for t in tops]
    total = sum(s * scalar(p, 3) for s, p in zip(scales, parts))
    return sum(s * p[:, :width] for s, p in zip(scales, parts)) / total


def slot_sums_kernel(chunks, phi_hbm, tokens_hbm, packed_ref, phi_ref, held, sems):
    slots, width = phi_ref.shape
    rows = tokens_hbm.shape[0] // chunks
    wide = width + LANES

    def copy(c):
        part = pl.ds(c * rows, rows)
        return pltpu.make_async_copy(tokens_hbm.at[part], held.at[part], sems.at[c])

    phi_copy = pltpu.make_async_copy(phi_hbm, phi_ref, sems.at[chunks])
    phi_copy.start()
    for c in range(chunks):
        copy(c).start()
    phi_copy.wait()
    spare = jnp.zeros((8 - slots % 8, width), F32)
    phi = jnp.concatenate([phi_ref[...].astype(F32), spare], axis=0).T.astype(BF16)
    tops, sums, totals = [], [], []

    def finish(c, by_token):
        part = pl.ds(c * rows, rows)
        logits = by_token.T[:slots]
        packed_ref[:, pl.ds(wide + c * rows, rows)] = logits
        top = jnp.max(logits, axis=1, keepdims=True)
        spread = jnp.exp(logits - top)
        tops.append(top)
        totals.append(jnp.sum(spread, axis=1, keepdims=True))
        sums.append(jnp.dot(spread.astype(BF16), held[part, :], preferred_element_type=F32))

    before = None
    for c in range(chunks):
        copy(c).wait()
        now = jnp.dot(held[pl.ds(c * rows, rows), :], phi, preferred_element_type=F32)
        if c:
            finish(c - 1, before)
        before = now
    finish(chunks - 1, before)
    top = functools.reduce(jnp.maximum, tops)
    scales = [jnp.exp(t - top) for t in tops]
    packed_ref[:, :width] = sum(s * v for s, v in zip(scales, sums))
    total = sum(s * v for s, v in zip(scales, totals))
    packed_ref[:, width:wide] = scalars(top, total)


def slot_sums(phi, tokens, chunks=4):
    (slots, width), count = phi.shape, tokens.shape[0]
    return pl.pallas_call(
        functools.partial(slot_sums_kernel, chunks),
        out_shape=jax.ShapeDtypeStruct((slots, width + LANES + count), F32),
        in_specs=[pl.BlockSpec(memory_space=pltpu.HBM)] * 2,
        out_specs=VMEM,
        scratch_shapes=[
            pltpu.VMEM(phi.shape, BF16),
            pltpu.VMEM(tokens.shape, BF16),
            pltpu.SemaphoreType.DMA((chunks + 1,)),
        ],
        compiler_params=params(16),
    )(in_hbm(phi), in_hbm(tokens))


def swapped(x):
    half = x.shape[0] // 2
    return jnp.concatenate([x[half:], x[:half]], axis=0)


def pair_kernel(own_ref, other_ref, sent_ref, both_ref, logits_ref):
    slots, wide = own_ref.shape[0], both_ref.shape[1]
    for i, ref in enumerate((own_ref, other_ref)):
        part = slice(i * slots, (i + 1) * slots)
        both_ref[part, :] = ref[:, :wide]
        logits_ref[part, :] = ref[:, wide:]
    sent_ref[...] = both_ref[...].astype(BF16)


def pair(own, other, wide):
    slots = 2 * own.shape[0]
    return pl.pallas_call(
        pair_kernel,
        out_shape=(
            jax.ShapeDtypeStruct((slots, wide), BF16),
            jax.ShapeDtypeStruct((slots, wide), F32),
            jax.ShapeDtypeStruct((slots, own.shape[1] - wide), F32),
        ),
        in_specs=[VMEM] * 2,
        out_specs=(VMEM,) * 3,
        cost_estimate=pl.CostEstimate(flops=10_000_000_000, bytes_accessed=0, transcendentals=0),
        compiler_params=params(4),
    )(own, other)


def gelu(v):
    return 0.5 * v * (1.0 + jnp.tanh(0.7978845608028654 * (v + 0.044715 * v * v * v)))


def experts_kernel(both_ref, *refs):
    *received, first_ref, second_ref, out_ref = refs
    slots, width = first_ref.shape[:2]
    slot_in = joined([both_ref[...]] + [swapped(r[...].astype(F32)) for r in received], width)
    for e in range(slots):
        x = jnp.concatenate([slot_in[e : e + 1], slot_in[slots + e : slots + e + 1]], axis=0)
        hidden = jnp.dot(x.astype(BF16), first_ref[e], preferred_element_type=F32)
        value = jnp.dot(gelu(hidden).astype(BF16), second_ref[e], preferred_element_type=F32)
        out_ref[e : e + 1, :] = value[:1]
        out_ref[slots + e : slots + e + 1, :] = value[1:]


def experts(both, received, w_in, w_out):
    return pl.pallas_call(
        experts_kernel,
        out_shape=jax.ShapeDtypeStruct((both.shape[0], w_in.shape[1]), F32),
        in_specs=[VMEM] * (len(received) + 3),
        out_specs=VMEM,
        compiler_params=params(4),
    )(both, *received, w_in, w_out)


def pack_kernel(chip_ref, *refs):
    *received, logits_ref, own_ref, other_ref = refs
    slots, width = own_ref.shape[0], chip_ref.shape[1]
    total = chip_ref[...]
    for r in received:
        total += swapped(r[...].astype(F32))
    total = total.astype(BF16).astype(F32)
    for out_ref, part in ((own_ref, slice(0, slots)), (other_ref, slice(slots, 2 * slots))):
        out_ref[:, :width] = total[part]
        out_ref[:, width:] = logits_ref[part, :]


def pack(chip, received, logits):
    slots, width = chip.shape
    shape = jax.ShapeDtypeStruct((slots // 2, width + logits.shape[1]), F32)
    return pl.pallas_call(
        pack_kernel,
        out_shape=(shape, shape),
        in_specs=[VMEM] * (len(received) + 2),
        out_specs=(VMEM, VMEM),
        compiler_params=params(4),
    )(chip, *received, logits)


def mix_kernel(chunks, *refs):
    *packed, out_hbm, rows_ref, sems = refs
    (count, width), group = rows_ref.shape, lax.axis_index("expert")
    rows = count // chunks
    values = jnp.concatenate([p[:, :width] for p in packed], axis=0).astype(BF16)
    everything = jnp.concatenate([p[:, width:] for p in packed], axis=0)
    logits = everything[:, :count]
    for g in range(1, len(packed)):
        logits = jnp.where(group == g, everything[:, g * count : (g + 1) * count], logits)
    weight = jnp.exp(logits - jnp.max(logits, axis=0, keepdims=True))
    weight = (weight / jnp.sum(weight, axis=0, keepdims=True)).astype(BF16)
    copies = []
    for c in range(chunks):
        part = pl.ds(c * rows, rows)
        rows_ref[part, :] = lax.dot_general(
            weight[:, c * rows : (c + 1) * rows],
            values,
            (((0,), (0,)), ((), ())),
            preferred_element_type=F32,
        ).astype(BF16)
        copies.append(pltpu.make_async_copy(rows_ref.at[part], out_hbm.at[part], sems.at[c]))
        copies[-1].start()
    for copy in copies:
        copy.wait()


def mix(packed, width, chunks=4):
    shape = ((packed[0].shape[1] - width) // len(packed), width)
    return pl.pallas_call(
        functools.partial(mix_kernel, chunks),
        out_shape=jax.ShapeDtypeStruct(shape, BF16),
        in_specs=[VMEM] * len(packed),
        out_specs=pl.BlockSpec(memory_space=pl.ANY),
        scratch_shapes=[pltpu.VMEM(shape, BF16), pltpu.SemaphoreType.DMA((chunks,))],
        compiler_params=params(8),
    )(*packed)


def on_device(sizes, tokens, phi, w_in, w_out):
    cores, seqs, groups = sizes
    width = tokens.shape[1]
    swap = partners(cores, 1)
    packed = slot_sums(phi.T, tokens)
    sent, both, logits = pair(packed, lax.ppermute(packed, "dp", swap), width + LANES)
    received = [exchange(sent, sizes, "seq", step) for step in middle_first(seqs)]
    partial = experts(both, received, w_in, w_out)
    chip = partial + swapped(lax.ppermute(partial, "dp", swap))
    sent = chip.astype(BF16)
    sums = [exchange(sent, sizes, "seq", step) for step in middle_first(seqs)]
    own, other = pack(chip, sums, logits)
    everyone = [own] + [exchange(other, sizes, "expert", step) for step in range(1, groups)]
    return mix(everyone, width)


def solution(mesh):
    sizes = tuple(mesh.shape[axis] for axis in ("dp", "seq", "expert"))
    placed = (
        P(("dp", "seq"), None),
        P(None, "expert"),
        P("expert", None, ("dp", "seq")),
        P("expert", ("dp", "seq"), None),
    )
    return jax.shard_map(
        functools.partial(on_device, sizes),
        mesh=mesh,
        in_specs=placed,
        out_specs=P(("dp", "seq", "expert"), None),
        check_vma=False,
    )
```

```python
import functools

import jax
import jax.numpy as jnp
from jax import lax
from jax.experimental import pallas as pl
from jax.experimental.pallas import tpu as pltpu
from jax.sharding import PartitionSpec as P

F32, BF16 = jnp.float32, jnp.bfloat16
LANES = 128
VMEM = pl.BlockSpec(memory_space=pltpu.VMEM)


def in_hbm(x):
    return pltpu.with_memory_space_constraint(x, pltpu.HBM)


def params(mib):
    return pltpu.CompilerParams(vmem_limit_bytes=mib << 20)


def partners(n, step):
    if n & (n - 1):
        return [(i, (i + step) % n) for i in range(n)]
    return [(i, i ^ step) for i in range(n)]


def around(ring, step):
    n = len(ring)
    return [(ring[i], ring[(i + step) % n]) for i in range(n)]


def halves_first(n):
    if n % 2 or n < 4:
        return list(range(n))
    inner = halves_first(n // 2)
    return [2 * i for i in inner] + [2 * i + 1 for i in inner]


def exchange(x, sizes, axis, moves):
    cores, seqs, groups = sizes
    to = dict(moves)
    pairs = []
    for core in range(cores):
        for seq in range(seqs):
            for group in range(groups):
                place = (core * seqs + seq) * groups + group
                target_seq, target_group = (to[seq], group) if axis == "seq" else (seq, to[group])
                pairs.append((place, ((core ^ 1) * seqs + target_seq) * groups + target_group))
    return lax.ppermute(x, ("dp", "seq", "expert"), pairs)


def scalars(top, total):
    lane = lax.broadcasted_iota(jnp.int32, (top.shape[0], LANES), 1)
    lanes = jnp.zeros(lane.shape, F32)
    for at, rest in ((0, top), (3, total)):
        for i in range(3):
            piece = rest.astype(BF16).astype(F32)
            lanes = jnp.where(lane == at + i, piece, lanes)
            rest = rest - piece
    return lanes


def joined(parts, width):
    def scalar(part, at):
        return sum(part[:, width + at + i : width + at + i + 1] for i in range(3))

    tops = [scalar(p, 0) for p in parts]
    top = functools.reduce(jnp.maximum, tops)
    scales = [jnp.exp(t - top) for t in tops]
    total = sum(s * scalar(p, 3) for s, p in zip(scales, parts))
    return sum(s * p[:, :width] for s, p in zip(scales, parts)) / total


def slot_sums_kernel(chunks, phi_hbm, tokens_hbm, packed_ref, phi_ref, held, sems):
    slots, width = phi_ref.shape
    rows = tokens_hbm.shape[0] // chunks
    wide = width + LANES

    def copy(c):
        part = pl.ds(c * rows, rows)
        return pltpu.make_async_copy(tokens_hbm.at[part], held.at[part], sems.at[c])

    phi_copy = pltpu.make_async_copy(phi_hbm, phi_ref, sems.at[chunks])
    phi_copy.start()
    for c in range(chunks):
        copy(c).start()
    phi_copy.wait()
    spare = jnp.zeros((8 - slots % 8, width), F32)
    phi = jnp.concatenate([phi_ref[...].astype(F32), spare], axis=0).T.astype(BF16)
    tops, sums, totals = [], [], []

    def finish(c, by_token):
        part = pl.ds(c * rows, rows)
        logits = by_token.T[:slots]
        packed_ref[:, pl.ds(wide + c * rows, rows)] = logits
        top = jnp.max(logits, axis=1, keepdims=True)
        spread = jnp.exp(logits - top)
        tops.append(top)
        totals.append(jnp.sum(spread, axis=1, keepdims=True))
        sums.append(finely(spread, held[part, :]))

    before = None
    for c in range(chunks):
        copy(c).wait()
        now = jnp.dot(held[pl.ds(c * rows, rows), :], phi, preferred_element_type=F32)
        if c:
            finish(c - 1, before)
        before = now
    finish(chunks - 1, before)
    top = functools.reduce(jnp.maximum, tops)
    scales = [jnp.exp(t - top) for t in tops]
    packed_ref[:, :width] = sum(s * v for s, v in zip(scales, sums))
    total = sum(s * v for s, v in zip(scales, totals))
    packed_ref[:, width:wide] = scalars(top, total)


def slot_sums(phi, tokens, chunks=4):
    (slots, width), count = phi.shape, tokens.shape[0]
    return pl.pallas_call(
        functools.partial(slot_sums_kernel, chunks),
        out_shape=jax.ShapeDtypeStruct((slots, width + LANES + count), F32),
        in_specs=[pl.BlockSpec(memory_space=pltpu.HBM)] * 2,
        out_specs=VMEM,
        scratch_shapes=[
            pltpu.VMEM(phi.shape, BF16),
            pltpu.VMEM(tokens.shape, BF16),
            pltpu.SemaphoreType.DMA((chunks + 1,)),
        ],
        compiler_params=params(16),
    )(in_hbm(phi), in_hbm(tokens))


def swapped(x):
    half = x.shape[0] // 2
    return jnp.concatenate([x[half:], x[:half]], axis=0)


def pair_kernel(own_ref, other_ref, sent_ref, both_ref, logits_ref):
    slots, wide = own_ref.shape[0], both_ref.shape[1]
    for i, ref in enumerate((own_ref, other_ref)):
        part = slice(i * slots, (i + 1) * slots)
        both_ref[part, :] = ref[:, :wide]
        logits_ref[part, :] = ref[:, wide:]
    sent_ref[...] = both_ref[...].astype(BF16)


def pair(own, other, wide):
    slots = 2 * own.shape[0]
    return pl.pallas_call(
        pair_kernel,
        out_shape=(
            jax.ShapeDtypeStruct((slots, wide), BF16),
            jax.ShapeDtypeStruct((slots, wide), F32),
            jax.ShapeDtypeStruct((slots, own.shape[1] - wide), F32),
        ),
        in_specs=[VMEM] * 2,
        out_specs=(VMEM,) * 3,
        cost_estimate=pl.CostEstimate(flops=10_000_000_000, bytes_accessed=0, transcendentals=0),
        compiler_params=params(4),
    )(own, other)


def finely(x, y):
    high = x.astype(BF16)
    low = (x - high.astype(F32)).astype(BF16)
    both = jnp.dot(jnp.concatenate([high, low], axis=0), y, preferred_element_type=F32)
    return both[: x.shape[0]] + both[x.shape[0] :]


def gelu(v):
    return 0.5 * v * (1.0 + jnp.tanh(0.7978845608028654 * (v + 0.044715 * v * v * v)))


def experts_kernel(both_ref, *refs):
    *received, first_ref, second_ref, out_ref = refs
    slots, width = first_ref.shape[:2]
    slot_in = joined([both_ref[...]] + [swapped(r[...].astype(F32)) for r in received], width)
    for e in range(slots):
        x = jnp.concatenate([slot_in[e : e + 1], slot_in[slots + e : slots + e + 1]], axis=0)
        value = finely(gelu(finely(x, first_ref[e])), second_ref[e])
        out_ref[e : e + 1, :] = value[:1]
        out_ref[slots + e : slots + e + 1, :] = value[1:]


def experts(both, received, w_in, w_out):
    return pl.pallas_call(
        experts_kernel,
        out_shape=jax.ShapeDtypeStruct((both.shape[0], w_in.shape[1]), F32),
        in_specs=[VMEM] * (len(received) + 3),
        out_specs=VMEM,
        compiler_params=params(4),
    )(both, *received, w_in, w_out)


def pack_kernel(chip_ref, *refs):
    *received, logits_ref, own_ref, other_ref = refs
    slots, width = own_ref.shape[0], chip_ref.shape[1]
    total = chip_ref[...]
    for r in received:
        total += swapped(r[...].astype(F32))
    total = total.astype(BF16).astype(F32)
    for out_ref, part in ((own_ref, slice(0, slots)), (other_ref, slice(slots, 2 * slots))):
        out_ref[:, :width] = total[part]
        out_ref[:, width:] = logits_ref[part, :]


def pack(chip, received, logits):
    slots, width = chip.shape
    shape = jax.ShapeDtypeStruct((slots // 2, width + logits.shape[1]), F32)
    return pl.pallas_call(
        pack_kernel,
        out_shape=(shape, shape),
        in_specs=[VMEM] * (len(received) + 2),
        out_specs=(VMEM, VMEM),
        compiler_params=params(4),
    )(chip, *received, logits)


def mix_kernel(chunks, *refs):
    *packed, out_hbm, rows_ref, sems = refs
    (count, width), group = rows_ref.shape, lax.axis_index("expert")
    rows = count // chunks
    values = jnp.concatenate([p[:, :width] for p in packed], axis=0).astype(BF16)
    everything = jnp.concatenate([p[:, width:] for p in packed], axis=0)
    logits = everything[:, :count]
    for g in range(1, len(packed)):
        logits = jnp.where(group == g, everything[:, g * count : (g + 1) * count], logits)
    weight = jnp.exp(logits - jnp.max(logits, axis=0, keepdims=True))
    weight = (weight / jnp.sum(weight, axis=0, keepdims=True)).astype(BF16)
    copies = []
    for c in range(chunks):
        part = pl.ds(c * rows, rows)
        rows_ref[part, :] = lax.dot_general(
            weight[:, c * rows : (c + 1) * rows],
            values,
            (((0,), (0,)), ((), ())),
            preferred_element_type=F32,
        ).astype(BF16)
        copies.append(pltpu.make_async_copy(rows_ref.at[part], out_hbm.at[part], sems.at[c]))
        copies[-1].start()
    for copy in copies:
        copy.wait()


def mix(packed, width, chunks=4):
    shape = ((packed[0].shape[1] - width) // len(packed), width)
    return pl.pallas_call(
        functools.partial(mix_kernel, chunks),
        out_shape=jax.ShapeDtypeStruct(shape, BF16),
        in_specs=[VMEM] * len(packed),
        out_specs=pl.BlockSpec(memory_space=pl.ANY),
        scratch_shapes=[pltpu.VMEM(shape, BF16), pltpu.SemaphoreType.DMA((chunks,))],
        compiler_params=params(8),
    )(*packed)


def on_device(sizes, tokens, phi, w_in, w_out):
    cores, seqs, groups = sizes
    width = tokens.shape[1]
    swap = partners(cores, 1)
    packed = slot_sums(phi.T, tokens)
    sent, both, logits = pair(packed, lax.ppermute(packed, "dp", swap), width + LANES)
    received = [
        exchange(sent, sizes, "seq", around(halves_first(seqs), step)) for step in [*range(2, seqs), 1]
    ]
    partial = experts(both, received, w_in, w_out)
    chip = partial + swapped(lax.ppermute(partial, "dp", swap))
    sent = chip.astype(BF16)
    sums = [
        exchange(sent, sizes, "seq", around(range(seqs), step)) for step in range(seqs - 1, 0, -1)
    ]
    own, other = pack(chip, sums, logits)
    order = sorted(range(1, groups), key=lambda step: (step != groups // 2, step))
    everyone = [own] + [exchange(other, sizes, "expert", partners(groups, step)) for step in order]
    return mix(everyone, width)


def solution(mesh):
    sizes = tuple(mesh.shape[axis] for axis in ("dp", "seq", "expert"))
    placed = (
        P(("dp", "seq"), None),
        P(None, "expert"),
        P("expert", None, ("dp", "seq")),
        P("expert", ("dp", "seq"), None),
    )
    return jax.shard_map(
        functools.partial(on_device, sizes),
        mesh=mesh,
        in_specs=placed,
        out_specs=P(("dp", "seq", "expert"), None),
        check_vma=False,
    )
```

```python
import functools

import jax
import jax.numpy as jnp
from jax import lax
from jax.experimental import pallas as pl
from jax.experimental.pallas import tpu as pltpu
from jax.sharding import PartitionSpec as P

F32, BF16 = jnp.float32, jnp.bfloat16
LANES = 128
VMEM = pl.BlockSpec(memory_space=pltpu.VMEM)


def in_hbm(x):
    return pltpu.with_memory_space_constraint(x, pltpu.HBM)


def params(mib):
    return pltpu.CompilerParams(vmem_limit_bytes=mib << 20)


def partners(n, step):
    if n & (n - 1):
        return [(i, (i + step) % n) for i in range(n)]
    return [(i, i ^ step) for i in range(n)]


def around(ring, step):
    n = len(ring)
    return [(ring[i], ring[(i + step) % n]) for i in range(n)]


def halves_first(n):
    if n % 2 or n < 4:
        return list(range(n))
    inner = halves_first(n // 2)
    return [2 * i for i in inner] + [2 * i + 1 for i in inner]


def exchange(x, sizes, axis, moves):
    cores, seqs, groups = sizes
    to = dict(moves)
    pairs = []
    for core in range(cores):
        for seq in range(seqs):
            for group in range(groups):
                place = (core * seqs + seq) * groups + group
                target_seq, target_group = (to[seq], group) if axis == "seq" else (seq, to[group])
                pairs.append((place, ((core ^ 1) * seqs + target_seq) * groups + target_group))
    return lax.ppermute(x, ("dp", "seq", "expert"), pairs)


def scalars(top, total):
    lane = lax.broadcasted_iota(jnp.int32, (top.shape[0], LANES), 1)
    lanes = jnp.zeros(lane.shape, F32)
    for at, rest in ((0, top), (3, total)):
        for i in range(3):
            piece = rest.astype(BF16).astype(F32)
            lanes = jnp.where(lane == at + i, piece, lanes)
            rest = rest - piece
    return lanes


def joined(parts, width):
    def scalar(part, at):
        return sum(part[:, width + at + i : width + at + i + 1] for i in range(3))

    tops = [scalar(p, 0) for p in parts]
    top = functools.reduce(jnp.maximum, tops)
    scales = [jnp.exp(t - top) for t in tops]
    total = sum(s * scalar(p, 3) for s, p in zip(scales, parts))
    return sum(s * p[:, :width] for s, p in zip(scales, parts)) / total


def slot_sums_kernel(chunks, phi_hbm, tokens_hbm, packed_ref, phi_ref, held, sems):
    slots, width = phi_ref.shape
    rows = tokens_hbm.shape[0] // chunks
    wide = width + LANES

    def copy(c):
        part = pl.ds(c * rows, rows)
        return pltpu.make_async_copy(tokens_hbm.at[part], held.at[part], sems.at[c])

    phi_copy = pltpu.make_async_copy(phi_hbm, phi_ref, sems.at[chunks])
    phi_copy.start()
    for c in range(chunks):
        copy(c).start()
    phi_copy.wait()
    spare = 8 - slots % 8
    by_slot = phi_ref[...].astype(F32)
    phi = jnp.concatenate([by_slot, jnp.zeros((spare, width), F32)], axis=0).T.astype(BF16)
    direct = rows // 4
    tops, sums, totals = [], [], []

    def finish(c, by_token):
        part = pl.ds(c * rows, rows)
        logits = by_token.T[:slots]
        packed_ref[:, pl.ds(wide + c * rows, rows)] = logits
        top = jnp.max(logits, axis=1, keepdims=True)
        spread = jnp.exp(logits - top)
        tops.append(top)
        totals.append(jnp.sum(spread, axis=1, keepdims=True))
        sums.append(finely(spread, held[part, :]))

    before = None
    for c in range(chunks):
        copy(c).wait()
        main = jnp.dot(held[pl.ds(c * rows, rows - direct), :], phi, preferred_element_type=F32)
        rest = held[pl.ds((c + 1) * rows - direct, direct), :].astype(F32)
        columns = [jnp.sum(rest * by_slot[s : s + 1], axis=1, keepdims=True) for s in range(slots)]
        columns.append(jnp.zeros((direct, spare), F32))
        now = jnp.concatenate([main, jnp.concatenate(columns, axis=1)], axis=0)
        if c:
            finish(c - 1, before)
        before = now
    finish(chunks - 1, before)
    top = functools.reduce(jnp.maximum, tops)
    scales = [jnp.exp(t - top) for t in tops]
    packed_ref[:, :width] = sum(s * v for s, v in zip(scales, sums))
    total = sum(s * v for s, v in zip(scales, totals))
    packed_ref[:, width:wide] = scalars(top, total)


def slot_sums(phi, tokens, chunks=4):
    (slots, width), count = phi.shape, tokens.shape[0]
    return pl.pallas_call(
        functools.partial(slot_sums_kernel, chunks),
        out_shape=jax.ShapeDtypeStruct((slots, width + LANES + count), F32),
        in_specs=[pl.BlockSpec(memory_space=pltpu.HBM)] * 2,
        out_specs=VMEM,
        scratch_shapes=[
            pltpu.VMEM(phi.shape, BF16),
            pltpu.VMEM(tokens.shape, BF16),
            pltpu.SemaphoreType.DMA((chunks + 1,)),
        ],
        compiler_params=params(16),
    )(in_hbm(phi), in_hbm(tokens))


def swapped(x):
    half = x.shape[0] // 2
    return jnp.concatenate([x[half:], x[:half]], axis=0)


def pair_kernel(own_ref, other_ref, sent_ref, both_ref, logits_ref):
    slots, wide = own_ref.shape[0], both_ref.shape[1]
    for i, ref in enumerate((own_ref, other_ref)):
        part = slice(i * slots, (i + 1) * slots)
        both_ref[part, :] = ref[:, :wide]
        logits_ref[part, :] = ref[:, wide:]
    sent_ref[...] = both_ref[...].astype(BF16)


def pair(own, other, wide):
    slots = 2 * own.shape[0]
    return pl.pallas_call(
        pair_kernel,
        out_shape=(
            jax.ShapeDtypeStruct((slots, wide), BF16),
            jax.ShapeDtypeStruct((slots, wide), F32),
            jax.ShapeDtypeStruct((slots, own.shape[1] - wide), F32),
        ),
        in_specs=[VMEM] * 2,
        out_specs=(VMEM,) * 3,
        cost_estimate=pl.CostEstimate(flops=10_000_000_000, bytes_accessed=0, transcendentals=0),
        compiler_params=params(4),
    )(own, other)


def finely(x, y):
    high = x.astype(BF16)
    low = (x - high.astype(F32)).astype(BF16)
    both = jnp.dot(jnp.concatenate([high, low], axis=0), y, preferred_element_type=F32)
    return both[: x.shape[0]] + both[x.shape[0] :]


def gelu(v):
    return 0.5 * v * (1.0 + jnp.tanh(0.7978845608028654 * (v + 0.044715 * v * v * v)))


def experts_kernel(both_ref, *refs):
    *received, first_ref, second_ref, out_ref = refs
    slots, width = first_ref.shape[:2]
    slot_in = joined([both_ref[...]] + [swapped(r[...].astype(F32)) for r in received], width)
    xs = [
        jnp.concatenate([slot_in[e : e + 1], slot_in[slots + e : slots + e + 1]], axis=0)
        for e in range(slots)
    ]
    hidden = [gelu(finely(x, first_ref[e])) for e, x in enumerate(xs)]
    for e in range(slots):
        value = finely(hidden[e], second_ref[e])
        out_ref[e : e + 1, :] = value[:1]
        out_ref[slots + e : slots + e + 1, :] = value[1:]


def experts(both, received, w_in, w_out):
    return pl.pallas_call(
        experts_kernel,
        out_shape=jax.ShapeDtypeStruct((both.shape[0], w_in.shape[1]), F32),
        in_specs=[VMEM] * (len(received) + 3),
        out_specs=VMEM,
        compiler_params=params(4),
    )(both, *received, w_in, w_out)


def pack_kernel(chip_ref, *refs):
    *received, logits_ref, own_ref, other_ref = refs
    slots, width = own_ref.shape[0], chip_ref.shape[1]
    total = chip_ref[...]
    for r in received:
        total += swapped(r[...].astype(F32))
    total = total.astype(BF16).astype(F32)
    for out_ref, part in ((own_ref, slice(0, slots)), (other_ref, slice(slots, 2 * slots))):
        out_ref[:, :width] = total[part]
        out_ref[:, width:] = logits_ref[part, :]


def pack(chip, received, logits):
    slots, width = chip.shape
    shape = jax.ShapeDtypeStruct((slots // 2, width + logits.shape[1]), F32)
    return pl.pallas_call(
        pack_kernel,
        out_shape=(shape, shape),
        in_specs=[VMEM] * (len(received) + 2),
        out_specs=(VMEM, VMEM),
        compiler_params=params(4),
    )(chip, *received, logits)


def mix_kernel(chunks, *refs):
    *packed, out_hbm, rows_ref, sems = refs
    (count, width), group = rows_ref.shape, lax.axis_index("expert")
    rows = count // chunks
    values = jnp.concatenate([p[:, :width] for p in packed], axis=0).astype(BF16)
    everything = jnp.concatenate([p[:, width:] for p in packed], axis=0)
    logits = everything[:, :count]
    for g in range(1, len(packed)):
        logits = jnp.where(group == g, everything[:, g * count : (g + 1) * count], logits)
    weight = jnp.exp(logits - jnp.max(logits, axis=0, keepdims=True))
    weight = (weight / jnp.sum(weight, axis=0, keepdims=True)).astype(BF16)
    copies = []
    for c in range(chunks):
        part = pl.ds(c * rows, rows)
        rows_ref[part, :] = lax.dot_general(
            weight[:, c * rows : (c + 1) * rows],
            values,
            (((0,), (0,)), ((), ())),
            preferred_element_type=F32,
        ).astype(BF16)
        copies.append(pltpu.make_async_copy(rows_ref.at[part], out_hbm.at[part], sems.at[c]))
        copies[-1].start()
    for copy in copies:
        copy.wait()


def mix(packed, width, chunks=4):
    shape = ((packed[0].shape[1] - width) // len(packed), width)
    return pl.pallas_call(
        functools.partial(mix_kernel, chunks),
        out_shape=jax.ShapeDtypeStruct(shape, BF16),
        in_specs=[VMEM] * len(packed),
        out_specs=pl.BlockSpec(memory_space=pl.ANY),
        scratch_shapes=[pltpu.VMEM(shape, BF16), pltpu.SemaphoreType.DMA((chunks,))],
        compiler_params=params(8),
    )(*packed)


def on_device(sizes, tokens, phi, w_in, w_out):
    cores, seqs, groups = sizes
    width = tokens.shape[1]
    swap = partners(cores, 1)
    packed = slot_sums(phi.T, tokens)
    sent, both, logits = pair(packed, lax.ppermute(packed, "dp", swap), width + LANES)
    received = [
        exchange(sent, sizes, "seq", around(halves_first(seqs), step)) for step in [*range(2, seqs), 1]
    ]
    partial = experts(both, received, w_in, w_out)
    chip = partial + swapped(lax.ppermute(partial, "dp", swap))
    sent = chip.astype(BF16)
    sums = [
        exchange(sent, sizes, "seq", around(range(seqs), step)) for step in range(seqs - 1, 0, -1)
    ]
    own, other = pack(chip, sums, logits)
    order = sorted(range(1, groups), key=lambda step: (step != groups // 2, step))
    everyone = [own] + [exchange(other, sizes, "expert", partners(groups, step)) for step in order]
    return mix(everyone, width)


def solution(mesh):
    sizes = tuple(mesh.shape[axis] for axis in ("dp", "seq", "expert"))
    placed = (
        P(("dp", "seq"), None),
        P(None, "expert"),
        P("expert", None, ("dp", "seq")),
        P("expert", ("dp", "seq"), None),
    )
    return jax.shard_map(
        functools.partial(on_device, sizes),
        mesh=mesh,
        in_specs=placed,
        out_specs=P(("dp", "seq", "expert"), None),
        check_vma=False,
    )
```

```python
import functools

import jax
import jax.numpy as jnp
from jax import lax
from jax.experimental import pallas as pl
from jax.experimental.pallas import tpu as pltpu
from jax.sharding import PartitionSpec as P

F32, BF16 = jnp.float32, jnp.bfloat16
LANES = 128
VMEM = pl.BlockSpec(memory_space=pltpu.VMEM)


def in_hbm(x):
    return pltpu.with_memory_space_constraint(x, pltpu.HBM)


def params(mib):
    return pltpu.CompilerParams(vmem_limit_bytes=mib << 20)


def partners(n, step):
    if n & (n - 1):
        return [(i, (i + step) % n) for i in range(n)]
    return [(i, i ^ step) for i in range(n)]


def around(ring, step):
    n = len(ring)
    return [(ring[i], ring[(i + step) % n]) for i in range(n)]


def halves_first(n):
    if n % 2 or n < 4:
        return list(range(n))
    inner = halves_first(n // 2)
    return [2 * i for i in inner] + [2 * i + 1 for i in inner]


def exchange(x, sizes, axis, moves):
    cores, seqs, groups = sizes
    to = dict(moves)
    pairs = []
    for core in range(cores):
        for seq in range(seqs):
            for group in range(groups):
                place = (core * seqs + seq) * groups + group
                target_seq, target_group = (to[seq], group) if axis == "seq" else (seq, to[group])
                pairs.append((place, ((core ^ 1) * seqs + target_seq) * groups + target_group))
    return lax.ppermute(x, ("dp", "seq", "expert"), pairs)


def pieces(x):
    found = []
    for _ in range(3):
        found.append(x.astype(BF16).astype(F32))
        x = x - found[-1]
    return found


def scalars(top, total):
    lane = lax.broadcasted_iota(jnp.int32, (top.shape[0], LANES), 1)
    lanes = jnp.zeros(lane.shape, F32)
    for i, piece in enumerate(pieces(top) + pieces(total)):
        lanes = jnp.where(lane == i, piece, lanes)
    return lanes


def joined(parts, width):
    def scalar(part, at):
        return sum(part[:, width + at + i : width + at + i + 1] for i in range(3))

    tops = [scalar(p, 0) for p in parts]
    top = functools.reduce(jnp.maximum, tops)
    scales = [jnp.exp(t - top) for t in tops]
    total = sum(s * scalar(p, 3) for s, p in zip(scales, parts))
    return sum(s * p[:, :width] for s, p in zip(scales, parts)) / total


def slot_sums_kernel(chunks, phi_hbm, tokens_hbm, packed_ref, phi_ref, held, sems):
    slots, width = phi_ref.shape
    rows = tokens_hbm.shape[0] // chunks
    wide = width + LANES

    def copy(c):
        part = pl.ds(c * rows, rows)
        return pltpu.make_async_copy(tokens_hbm.at[part], held.at[part], sems.at[c])

    phi_copy = pltpu.make_async_copy(phi_hbm, phi_ref, sems.at[chunks])
    phi_copy.start()
    for c in range(chunks):
        copy(c).start()
    phi_copy.wait()
    spare = 8 - slots % 8
    by_slot = phi_ref[...].astype(F32)
    phi = jnp.concatenate([by_slot, jnp.zeros((spare, width), F32)], axis=0).T.astype(BF16)
    direct = rows // 4
    tops, sums, totals = [], [], []

    def finish(c, by_token):
        part = pl.ds(c * rows, rows)
        logits = by_token.T[:slots]
        packed_ref[:, pl.ds(wide + c * rows, rows)] = logits
        top = jnp.max(logits, axis=1, keepdims=True)
        spread = jnp.exp(logits - top)
        tops.append(top)
        totals.append(jnp.sum(spread, axis=1, keepdims=True))
        sums.append(finely(spread, held[part, :]))

    before = None
    for c in range(chunks):
        copy(c).wait()
        main = jnp.dot(held[pl.ds(c * rows, rows - direct), :], phi, preferred_element_type=F32)
        rest = held[pl.ds((c + 1) * rows - direct, direct), :].astype(F32)
        columns = [jnp.sum(rest * by_slot[s : s + 1], axis=1, keepdims=True) for s in range(slots)]
        columns.append(jnp.zeros((direct, spare), F32))
        now = jnp.concatenate([main, jnp.concatenate(columns, axis=1)], axis=0)
        if c:
            finish(c - 1, before)
        before = now
    finish(chunks - 1, before)
    top = functools.reduce(jnp.maximum, tops)
    scales = [jnp.exp(t - top) for t in tops]
    packed_ref[:, :width] = sum(s * v for s, v in zip(scales, sums))
    total = sum(s * v for s, v in zip(scales, totals))
    packed_ref[:, width:wide] = scalars(top, total)


def slot_sums(phi, tokens, chunks=4):
    (slots, width), count = phi.shape, tokens.shape[0]
    return pl.pallas_call(
        functools.partial(slot_sums_kernel, chunks),
        out_shape=jax.ShapeDtypeStruct((slots, width + LANES + count), F32),
        in_specs=[pl.BlockSpec(memory_space=pltpu.HBM)] * 2,
        out_specs=VMEM,
        scratch_shapes=[
            pltpu.VMEM(phi.shape, BF16),
            pltpu.VMEM(tokens.shape, BF16),
            pltpu.SemaphoreType.DMA((chunks + 1,)),
        ],
        compiler_params=params(16),
    )(in_hbm(phi), in_hbm(tokens))


def swapped(x):
    half = x.shape[0] // 2
    return jnp.concatenate([x[half:], x[:half]], axis=0)


def pair_kernel(own_ref, other_ref, sent_ref, both_ref, logits_ref):
    slots, wide = own_ref.shape[0], both_ref.shape[1]
    for i, ref in enumerate((own_ref, other_ref)):
        part = slice(i * slots, (i + 1) * slots)
        both_ref[part, :] = ref[:, :wide]
        logits_ref[part, :] = ref[:, wide:]
    sent_ref[...] = both_ref[...].astype(BF16)


def pair(own, other, wide):
    slots = 2 * own.shape[0]
    return pl.pallas_call(
        pair_kernel,
        out_shape=(
            jax.ShapeDtypeStruct((slots, wide), BF16),
            jax.ShapeDtypeStruct((slots, wide), F32),
            jax.ShapeDtypeStruct((slots, own.shape[1] - wide), F32),
        ),
        in_specs=[VMEM] * 2,
        out_specs=(VMEM,) * 3,
        cost_estimate=pl.CostEstimate(flops=10_000_000_000, bytes_accessed=0, transcendentals=0),
        compiler_params=params(4),
    )(own, other)


def finely(x, y):
    high = x.astype(BF16)
    low = (x - high.astype(F32)).astype(BF16)
    both = jnp.dot(jnp.concatenate([high, low], axis=0), y, preferred_element_type=F32)
    return both[: x.shape[0]] + both[x.shape[0] :]


def gelu(v):
    return 0.5 * v * (1.0 + jnp.tanh(0.7978845608028654 * (v + 0.044715 * v * v * v)))


def experts_kernel(both_ref, *refs):
    *received, first_ref, second_ref, out_ref = refs
    slots, width = first_ref.shape[:2]
    slot_in = joined([both_ref[...]] + [swapped(r[...].astype(F32)) for r in received], width)
    xs = [
        jnp.concatenate([slot_in[e : e + 1], slot_in[slots + e : slots + e + 1]], axis=0)
        for e in range(slots)
    ]
    hidden = [gelu(finely(x, first_ref[e])) for e, x in enumerate(xs)]
    for e in range(slots):
        value = finely(hidden[e], second_ref[e])
        out_ref[e : e + 1, :] = value[:1]
        out_ref[slots + e : slots + e + 1, :] = value[1:]


def experts(both, received, w_in, w_out):
    return pl.pallas_call(
        experts_kernel,
        out_shape=jax.ShapeDtypeStruct((both.shape[0], w_in.shape[1]), F32),
        in_specs=[VMEM] * (len(received) + 3),
        out_specs=VMEM,
        compiler_params=params(4),
    )(both, *received, w_in, w_out)


def pack_kernel(places, chip_ref, *refs):
    received, (logits_ref, own_ref, *out_refs) = refs[: -len(places) - 2], refs[-len(places) - 2 :]
    slots, width = own_ref.shape[0], chip_ref.shape[1]
    rows, group = own_ref.shape[1] - width, lax.axis_index("expert")
    total = chip_ref[...]
    for r in received:
        total += swapped(r[...].astype(F32))

    def chosen(part, to):
        logits = logits_ref[part, to[0] * rows : (to[0] + 1) * rows]
        for g in range(1, len(to)):
            here = logits_ref[part, to[g] * rows : (to[g] + 1) * rows]
            logits = jnp.where(group == g, here, logits)
        return logits

    own, other = slice(0, slots), slice(slots, 2 * slots)
    own_ref[:, :width] = total[own]
    own_ref[:, width:] = chosen(own, range(len(places) + 1))
    for out_ref, pairs in zip(out_refs, places):
        logits = pieces(chosen(other, dict(pairs)))
        out_ref[...] = jnp.concatenate([total[other]] + logits, axis=1).astype(BF16)


def pack(chip, received, logits, places):
    slots, width = chip.shape[0] // 2, chip.shape[1]
    rows = logits.shape[1] // (len(places) + 1)
    sent = jax.ShapeDtypeStruct((slots, width + 3 * rows), BF16)
    return pl.pallas_call(
        functools.partial(pack_kernel, places),
        out_shape=[jax.ShapeDtypeStruct((slots, width + rows), F32)] + [sent] * len(places),
        in_specs=[VMEM] * (len(received) + 2),
        out_specs=[VMEM] * (len(places) + 1),
        compiler_params=params(4),
    )(chip, *received, logits)


def mix_kernel(chunks, own_ref, *refs):
    *received, out_hbm, rows_ref, sems = refs
    count, width = rows_ref.shape
    rows = count // chunks
    values, logits = [own_ref[:, :width]], [own_ref[:, width:]]
    for r in received:
        part = r[...].astype(F32)
        values.append(part[:, :width])
        logits.append(sum(part[:, width + i * count : width + (i + 1) * count] for i in range(3)))
    values = jnp.concatenate(values, axis=0).astype(BF16)
    logits = jnp.concatenate(logits, axis=0)
    weight = jnp.exp(logits - jnp.max(logits, axis=0, keepdims=True))
    weight = (weight / jnp.sum(weight, axis=0, keepdims=True)).astype(BF16)
    copies = []
    for c in range(chunks):
        part = pl.ds(c * rows, rows)
        rows_ref[part, :] = lax.dot_general(
            weight[:, c * rows : (c + 1) * rows],
            values,
            (((0,), (0,)), ((), ())),
            preferred_element_type=F32,
        ).astype(BF16)
        copies.append(pltpu.make_async_copy(rows_ref.at[part], out_hbm.at[part], sems.at[c]))
        copies[-1].start()
    for copy in copies:
        copy.wait()


def mix(own, received, width, chunks=4):
    shape = (own.shape[1] - width, width)
    return pl.pallas_call(
        functools.partial(mix_kernel, chunks),
        out_shape=jax.ShapeDtypeStruct(shape, BF16),
        in_specs=[VMEM] * (len(received) + 1),
        out_specs=pl.BlockSpec(memory_space=pl.ANY),
        scratch_shapes=[pltpu.VMEM(shape, BF16), pltpu.SemaphoreType.DMA((chunks,))],
        compiler_params=params(8),
    )(own, *received)


def on_device(sizes, tokens, phi, w_in, w_out):
    cores, seqs, groups = sizes
    width = tokens.shape[1]
    swap = partners(cores, 1)
    packed = slot_sums(phi.T, tokens)
    sent, both, logits = pair(packed, lax.ppermute(packed, "dp", swap), width + LANES)
    received = [
        exchange(sent, sizes, "seq", around(halves_first(seqs), step)) for step in [*range(2, seqs), 1]
    ]
    partial = experts(both, received, w_in, w_out)
    chip = partial + swapped(lax.ppermute(partial, "dp", swap))
    sent = chip.astype(BF16)
    sums = [
        exchange(sent, sizes, "seq", around(range(seqs), step)) for step in range(seqs - 1, 0, -1)
    ]
    order = [groups - 1, *range(1, groups - 1)]
    places = [partners(groups, step) for step in order]
    own, *others = pack(chip, sums, logits, places)
    everyone = [exchange(x, sizes, "expert", moves) for x, moves in zip(others, places)]
    return mix(own, everyone, width)


def solution(mesh):
    sizes = tuple(mesh.shape[axis] for axis in ("dp", "seq", "expert"))
    placed = (
        P(("dp", "seq"), None),
        P(None, "expert"),
        P("expert", None, ("dp", "seq")),
        P("expert", ("dp", "seq"), None),
    )
    return jax.shard_map(
        functools.partial(on_device, sizes),
        mesh=mesh,
        in_specs=placed,
        out_specs=P(("dp", "seq", "expert"), None),
        check_vma=False,
    )
```

```python
import functools

import jax
import jax.numpy as jnp
from jax import lax
from jax.experimental import pallas as pl
from jax.experimental.pallas import tpu as pltpu
from jax.sharding import PartitionSpec as P

F32, BF16 = jnp.float32, jnp.bfloat16
LANES = 128
VMEM = pl.BlockSpec(memory_space=pltpu.VMEM)


def in_hbm(x):
    return pltpu.with_memory_space_constraint(x, pltpu.HBM)


def params(mib):
    return pltpu.CompilerParams(vmem_limit_bytes=mib << 20)


def partners(n, step):
    if n & (n - 1):
        return [(i, (i + step) % n) for i in range(n)]
    return [(i, i ^ step) for i in range(n)]


def around(ring, step):
    n = len(ring)
    return [(ring[i], ring[(i + step) % n]) for i in range(n)]


def halves_first(n):
    if n % 2 or n < 4:
        return list(range(n))
    inner = halves_first(n // 2)
    return [2 * i for i in inner] + [2 * i + 1 for i in inner]


def exchange(x, sizes, axis, moves):
    cores, seqs, groups = sizes
    to = dict(moves)
    pairs = []
    for core in range(cores):
        for seq in range(seqs):
            for group in range(groups):
                place = (core * seqs + seq) * groups + group
                target_seq, target_group = (to[seq], group) if axis == "seq" else (seq, to[group])
                pairs.append((place, ((core ^ 1) * seqs + target_seq) * groups + target_group))
    return lax.ppermute(x, ("dp", "seq", "expert"), pairs)


def pieces(x):
    found = []
    for _ in range(3):
        found.append(x.astype(BF16).astype(F32))
        x = x - found[-1]
    return found


def scalars(top, total):
    lane = lax.broadcasted_iota(jnp.int32, (top.shape[0], LANES), 1)
    lanes = jnp.zeros(lane.shape, F32)
    for i, piece in enumerate(pieces(top) + pieces(total)):
        lanes = jnp.where(lane == i, piece, lanes)
    return lanes


def joined(parts, width):
    def scalar(part, at):
        return sum(part[:, width + at + i : width + at + i + 1] for i in range(3))

    tops = [scalar(p, 0) for p in parts]
    top = functools.reduce(jnp.maximum, tops)
    scales = [jnp.exp(t - top) for t in tops]
    total = sum(s * scalar(p, 3) for s, p in zip(scales, parts))
    return sum(s / total * p[:, :width] for s, p in zip(scales, parts))


def slot_sums_kernel(chunks, phi_hbm, tokens_hbm, packed_ref, phi_ref, held, sems):
    slots, width = phi_ref.shape
    rows = tokens_hbm.shape[0] // chunks
    wide = width + LANES

    def copy(c):
        part = pl.ds(c * rows, rows)
        return pltpu.make_async_copy(tokens_hbm.at[part], held.at[part], sems.at[c])

    phi_copy = pltpu.make_async_copy(phi_hbm, phi_ref, sems.at[chunks])
    phi_copy.start()
    for c in range(chunks):
        copy(c).start()
    phi_copy.wait()
    spare = 8 - slots % 8
    by_slot = phi_ref[...].astype(F32)
    phi = jnp.concatenate([by_slot, jnp.zeros((spare, width), F32)], axis=0).T.astype(BF16)
    direct = rows // 4
    tops, sums, totals = [], [], []

    def finish(c, by_token):
        part = pl.ds(c * rows, rows)
        logits = by_token.T[:slots]
        packed_ref[:, pl.ds(wide + c * rows, rows)] = logits
        top = jnp.max(logits, axis=1, keepdims=True)
        spread = jnp.exp(logits - top)
        tops.append(top)
        totals.append(jnp.sum(spread, axis=1, keepdims=True))
        sums.append(finely(spread, held[part, :]))

    before = None
    for c in range(chunks):
        copy(c).wait()
        main = jnp.dot(held[pl.ds(c * rows, rows - direct), :], phi, preferred_element_type=F32)
        rest = held[pl.ds((c + 1) * rows - direct, direct), :].astype(F32)
        columns = [jnp.sum(rest * by_slot[s : s + 1], axis=1, keepdims=True) for s in range(slots)]
        columns.append(jnp.zeros((direct, spare), F32))
        now = jnp.concatenate([main, jnp.concatenate(columns, axis=1)], axis=0)
        if c:
            finish(c - 1, before)
        before = now
    finish(chunks - 1, before)
    top = functools.reduce(jnp.maximum, tops)
    scales = [jnp.exp(t - top) for t in tops]
    packed_ref[:, :width] = sum(s * v for s, v in zip(scales, sums))
    total = sum(s * v for s, v in zip(scales, totals))
    packed_ref[:, width:wide] = scalars(top, total)


def slot_sums(phi, tokens, chunks=4):
    (slots, width), count = phi.shape, tokens.shape[0]
    return pl.pallas_call(
        functools.partial(slot_sums_kernel, chunks),
        out_shape=jax.ShapeDtypeStruct((slots, width + LANES + count), F32),
        in_specs=[pl.BlockSpec(memory_space=pltpu.HBM)] * 2,
        out_specs=VMEM,
        scratch_shapes=[
            pltpu.VMEM(phi.shape, BF16),
            pltpu.VMEM(tokens.shape, BF16),
            pltpu.SemaphoreType.DMA((chunks + 1,)),
        ],
        compiler_params=params(16),
    )(in_hbm(phi), in_hbm(tokens))


def swapped(x):
    half = x.shape[0] // 2
    return jnp.concatenate([x[half:], x[:half]], axis=0)


def pair_kernel(own_ref, other_ref, sent_ref, both_ref, logits_ref):
    slots, wide = own_ref.shape[0], both_ref.shape[1]
    for i, ref in enumerate((own_ref, other_ref)):
        part = slice(i * slots, (i + 1) * slots)
        both_ref[part, :] = ref[:, :wide]
        logits_ref[part, :] = ref[:, wide:]
    sent_ref[...] = both_ref[...].astype(BF16)


def pair(own, other, wide):
    slots = 2 * own.shape[0]
    return pl.pallas_call(
        pair_kernel,
        out_shape=(
            jax.ShapeDtypeStruct((slots, wide), BF16),
            jax.ShapeDtypeStruct((slots, wide), F32),
            jax.ShapeDtypeStruct((slots, own.shape[1] - wide), F32),
        ),
        in_specs=[VMEM] * 2,
        out_specs=(VMEM,) * 3,
        cost_estimate=pl.CostEstimate(flops=10_000_000_000, bytes_accessed=0, transcendentals=0),
        compiler_params=params(4),
    )(own, other)


def finely(x, y):
    high = x.astype(BF16)
    low = (x - high.astype(F32)).astype(BF16)
    both = jnp.dot(jnp.concatenate([high, low], axis=0), y, preferred_element_type=F32)
    return both[: x.shape[0]] + both[x.shape[0] :]


def gelu(v):
    return 0.5 * v * (1.0 + jnp.tanh(0.7978845608028654 * (v + 0.044715 * v * v * v)))


def experts_kernel(both_ref, *refs):
    *received, first_ref, second_ref, out_ref = refs
    slots, width = first_ref.shape[:2]
    slot_in = joined([both_ref[...]] + [swapped(r[...].astype(F32)) for r in received], width)
    xs = [
        jnp.concatenate([slot_in[e : e + 1], slot_in[slots + e : slots + e + 1]], axis=0)
        for e in range(slots)
    ]
    hidden = [gelu(finely(x, first_ref[e])) for e, x in enumerate(xs)]
    for e in range(slots):
        value = finely(hidden[e], second_ref[e])
        out_ref[e : e + 1, :] = value[:1]
        out_ref[slots + e : slots + e + 1, :] = value[1:]


def experts(both, received, w_in, w_out):
    return pl.pallas_call(
        experts_kernel,
        out_shape=jax.ShapeDtypeStruct((both.shape[0], w_in.shape[1]), F32),
        in_specs=[VMEM] * (len(received) + 3),
        out_specs=VMEM,
        compiler_params=params(4),
    )(both, *received, w_in, w_out)


def pack_kernel(places, chip_ref, *refs):
    received, (logits_ref, own_ref, *out_refs) = refs[: -len(places) - 2], refs[-len(places) - 2 :]
    slots, width = own_ref.shape[0], chip_ref.shape[1]
    rows, group = own_ref.shape[1] - width, lax.axis_index("expert")
    total = chip_ref[...]
    for r in received:
        total += swapped(r[...].astype(F32))

    def chosen(part, to):
        logits = logits_ref[part, to[0] * rows : (to[0] + 1) * rows]
        for g in range(1, len(to)):
            here = logits_ref[part, to[g] * rows : (to[g] + 1) * rows]
            logits = jnp.where(group == g, here, logits)
        return logits

    own, other = slice(0, slots), slice(slots, 2 * slots)
    own_ref[:, :width] = total[own]
    own_ref[:, width:] = chosen(own, range(len(places) + 1))
    for out_ref, pairs in zip(out_refs, places):
        logits = pieces(chosen(other, dict(pairs)))
        out_ref[...] = jnp.concatenate([total[other]] + logits, axis=1).astype(BF16)


def pack(chip, received, logits, places):
    slots, width = chip.shape[0] // 2, chip.shape[1]
    rows = logits.shape[1] // (len(places) + 1)
    sent = jax.ShapeDtypeStruct((slots, width + 3 * rows), BF16)
    return pl.pallas_call(
        functools.partial(pack_kernel, places),
        out_shape=[jax.ShapeDtypeStruct((slots, width + rows), F32)] + [sent] * len(places),
        in_specs=[VMEM] * (len(received) + 2),
        out_specs=[VMEM] * (len(places) + 1),
        compiler_params=params(4),
    )(chip, *received, logits)


def mix_kernel(chunks, own_ref, *refs):
    *received, out_hbm, rows_ref, sems = refs
    count, width = rows_ref.shape
    rows = count // chunks
    values, logits = [own_ref[:, :width]], [own_ref[:, width:]]
    for r in received:
        part = r[...].astype(F32)
        values.append(part[:, :width])
        logits.append(sum(part[:, width + i * count : width + (i + 1) * count] for i in range(3)))
    values = jnp.concatenate(values, axis=0).astype(BF16)
    logits = jnp.concatenate(logits, axis=0)
    weight = jnp.exp(logits - jnp.max(logits, axis=0, keepdims=True))
    weight = (weight / jnp.sum(weight, axis=0, keepdims=True)).astype(BF16)
    copies = []
    for c in range(chunks):
        part = pl.ds(c * rows, rows)
        rows_ref[part, :] = lax.dot_general(
            weight[:, c * rows : (c + 1) * rows],
            values,
            (((0,), (0,)), ((), ())),
            preferred_element_type=F32,
        ).astype(BF16)
        copies.append(pltpu.make_async_copy(rows_ref.at[part], out_hbm.at[part], sems.at[c]))
        copies[-1].start()
    for copy in copies:
        copy.wait()


def mix(own, received, width, chunks=4):
    shape = (own.shape[1] - width, width)
    return pl.pallas_call(
        functools.partial(mix_kernel, chunks),
        out_shape=jax.ShapeDtypeStruct(shape, BF16),
        in_specs=[VMEM] * (len(received) + 1),
        out_specs=pl.BlockSpec(memory_space=pl.ANY),
        scratch_shapes=[pltpu.VMEM(shape, BF16), pltpu.SemaphoreType.DMA((chunks,))],
        compiler_params=params(8),
    )(own, *received)


def on_device(sizes, tokens, phi, w_in, w_out):
    cores, seqs, groups = sizes
    width = tokens.shape[1]
    swap = partners(cores, 1)
    packed = slot_sums(phi.T, tokens)
    sent, both, logits = pair(packed, lax.ppermute(packed, "dp", swap), width + LANES)
    received = [
        exchange(sent, sizes, "seq", around(halves_first(seqs), step)) for step in [*range(2, seqs), 1]
    ]
    partial = experts(both, received, w_in, w_out)
    chip = partial + swapped(lax.ppermute(partial, "dp", swap))
    sent = chip.astype(BF16)
    sums = [
        exchange(sent, sizes, "seq", around(range(seqs), step)) for step in range(seqs - 1, 0, -1)
    ]
    order = [groups - 1, *range(1, groups - 1)]
    places = [partners(groups, step) for step in order]
    own, *others = pack(chip, sums, logits, places)
    everyone = [exchange(x, sizes, "expert", moves) for x, moves in zip(others, places)]
    return mix(own, everyone, width)


def solution(mesh):
    sizes = tuple(mesh.shape[axis] for axis in ("dp", "seq", "expert"))
    placed = (
        P(("dp", "seq"), None),
        P(None, "expert"),
        P("expert", None, ("dp", "seq")),
        P("expert", ("dp", "seq"), None),
    )
    return jax.shard_map(
        functools.partial(on_device, sizes),
        mesh=mesh,
        in_specs=placed,
        out_specs=P(("dp", "seq", "expert"), None),
        check_vma=False,
    )
```
